32 devices in a mesh: seq: 32 (over z, y, x, core), mp: 1.
Axes of the slice: x: 2, y: 2, z: 4, core: 2. Of those that a mesh axis runs over, the one named last changes fastest.
Arguments:
- states: bfloat16 [8192, 2560], P('seq'), may hold values from -8 to 8
- query_rows: bfloat16 [8192, 1280], P('seq', 'mp'), may hold values from -8 to 8
- key_rows: bfloat16 [8192, 1280], P('seq', 'mp'), may hold values from -8 to 8
- value_rows: bfloat16 [8192, 1280], P('seq', 'mp'), may hold values from -6 to 6
- out_proj: bfloat16 [1280, 2560], P('mp'), may hold values from -0.15625 to 0.15625
- norm_gain: float32 [2560], replicated, may hold values from 0.1 to 1.9
- up_proj: bfloat16 [2560, 5120], P(None, 'mp'), may hold values from -0.125 to 0.125
- down_proj: bfloat16 [5120, 2560], P('mp', 'seq'), may hold values from -0.078125 to 0.078125
Outputs:
- layer_out: bfloat16 [8192, 2560], P('seq', 'mp')
The draws below stay inside these ranges and needn't reach their ends.
All inputs are finite; a program needn't handle non-finite values.
Results may differ from the reference program's by a relative error of at most 0.008.
Values may be sent and summed in bfloat16 or wider, within the bound.
A program may use at most 192 MiB of HBM per device.

```python
import functools
import math
import jax
import jax.numpy as jnp
from jax import lax

D = 2560
HEADS = 16
HEAD_DIM = 80
FF = 5120
SEG0 = 2048
TOKENS = 8192
LEVELS = 3


def base_rows(key, salt_value):
    noise_key = jax.random.fold_in(key, salt_value)
    return 1.6 * jax.random.normal(noise_key, (TOKENS, HEADS, HEAD_DIM), jnp.float32)


def draw_query_rows(key, part):
    drawn = base_rows(key, 11)
    return jnp.clip(drawn, -8.0, 8.0).reshape(TOKENS, HEADS * HEAD_DIM).astype(jnp.bfloat16)


def draw_key_rows(key, part):
    drawn = base_rows(key, 12)
    return jnp.clip(drawn, -8.0, 8.0).reshape(TOKENS, HEADS * HEAD_DIM).astype(jnp.bfloat16)


def draw_states(key, part):
    row_scale = jnp.exp(jax.random.uniform(jax.random.fold_in(key, 21), (TOKENS, 1), jnp.float32, math.log(0.3), math.log(3.0)))
    col_scale = jnp.exp(jax.random.uniform(jax.random.fold_in(key, 22), (1, D), jnp.float32, math.log(0.3), math.log(3.0)))
    noise = jax.random.normal(jax.random.fold_in(key, 23), (TOKENS, D), jnp.float32)
    return jnp.clip(0.5 * noise * row_scale * col_scale, -8.0, 8.0).astype(jnp.bfloat16)


def shard_levels(own_key, dims, cuts, smallest, top_value):
    def one(position, shards_of):
        draws = jax.random.uniform(jax.random.fold_in(jax.random.fold_in(own_key, 6), position), (shards_of,), jnp.float32, smallest / len(cuts), top_value / len(cuts))
        return jnp.repeat(jnp.exp(draws), dims[position] // shards_of).reshape((-1,) + (1,) * (len(dims) - position - 1))

    factor_of = one(*cuts[0])
    for cut in cuts[1:]:
        factor_of = factor_of * one(*cut)
    return factor_of


def centred(own_key, dims, spread, most, pieces=(), kind=jnp.bfloat16):
    array = spread * jax.random.normal(own_key, dims, jnp.float32)
    if pieces:
        array = array * shard_levels(own_key, dims, pieces, -0.22, 0.18)
    return jnp.clip(array, -most, most).astype(kind)


def setup_inputs(seed: int = 0) -> dict:
    splits = jax.random.split(jax.random.key(seed), 9)
    return {
        "states": draw_states(jax.random.fold_in(splits[8], 71), 0),
        "query_rows": draw_query_rows(jax.random.fold_in(splits[8], 71), 0),
        "key_rows": draw_key_rows(jax.random.fold_in(splits[8], 71), 0),
        "value_rows": centred(splits[3], (TOKENS, HEADS * HEAD_DIM), 1.0, 6.0, ((0, 32),)),
        "out_proj": centred(splits[4], (HEADS * HEAD_DIM, D), (HEADS * HEAD_DIM) ** -0.5, 0.15625),
        "norm_gain": jnp.clip(1.0 + 0.18 * jax.random.normal(splits[5], (D,), jnp.float32), 0.1, 1.9),
        "up_proj": centred(splits[6], (D, FF), D ** -0.5, 0.125),
        "down_proj": centred(splits[7], (FF, D), FF ** -0.5, 0.078125, ((1, 32),)),
    }


def select_rows(source, stride, offsets):
    leading = source.shape[:-2]
    row_count, col_count = (source.shape[-2], source.shape[-1])
    grouped = source.reshape(leading + (row_count // stride, stride, col_count))
    picked = jnp.arange(stride)[:, None] == offsets[None, :]
    return lax.optimization_barrier(jnp.sum(jnp.where(picked, grouped, jnp.zeros((), source.dtype)), axis=-2)).astype(source.dtype)

def spread_rows(source, stride, offsets):
    row_count, col_count = source.shape
    picked = jnp.arange(stride)[:, None] == offsets[None, :]
    placed = jnp.where(picked[None], source[:, None, :], jnp.zeros((), source.dtype))
    return placed.reshape(row_count * stride, col_count)

def segment_attend(query_seg, key_seg, value_seg):
    row_count, col_count = query_seg.shape
    head_count = col_count // HEAD_DIM
    query_heads = query_seg.astype(jnp.float32).reshape(row_count, head_count, HEAD_DIM)
    key_heads = key_seg.astype(jnp.float32).reshape(row_count, head_count, HEAD_DIM)
    value_heads = value_seg.astype(jnp.float32).reshape(row_count, head_count, HEAD_DIM)
    scores = jnp.einsum('qhd,khd->hqk', query_heads, key_heads) * HEAD_DIM ** (-0.5)
    causal = jnp.arange(row_count)[None, :] <= jnp.arange(row_count)[:, None]
    scores = jnp.where(causal[None], scores, -1e+30)
    row_peak = lax.optimization_barrier(jnp.max(scores, axis=-1))
    shifted_exp = jnp.exp(scores - row_peak[..., None])
    row_total = lax.optimization_barrier(jnp.sum(shifted_exp, axis=-1))
    rounded = lax.optimization_barrier(shifted_exp.astype(jnp.bfloat16)).astype(jnp.float32)
    weighted = jnp.einsum('hqk,khd->qhd', rounded, value_heads)
    return (row_peak.T, row_total.T, weighted.reshape(row_count, col_count))

def reference(states, query_rows, key_rows, value_rows, out_proj, norm_gain, up_proj, down_proj):
    col_total = HEADS * HEAD_DIM
    col_heads = jnp.arange(col_total) // HEAD_DIM
    head_ids = jnp.arange(HEADS)
    tier_peaks, tier_totals, tier_sums, tier_masks = ([], [], [], [])
    for tier_idx in range(LEVELS):
        stride = 2 ** tier_idx
        offsets = col_heads % stride
        picks = tuple((select_rows(source, stride, offsets).reshape(-1, SEG0, col_total) for source in (query_rows, key_rows, value_rows)))
        row_peak, row_total, weighted = lax.map(lambda trio: segment_attend(trio[0], trio[1], trio[2]), picks)
        head_offsets = head_ids % stride
        tier_peaks.append(spread_rows(row_peak.reshape(-1, HEADS), stride, head_offsets))
        tier_totals.append(spread_rows(row_total.reshape(-1, HEADS), stride, head_offsets))
        tier_sums.append(spread_rows(weighted.reshape(-1, col_total), stride, offsets))
        tier_masks.append(spread_rows(jnp.ones((TOKENS // stride, HEADS), jnp.float32), stride, head_offsets) > 0.5)
    masked_peaks = [jnp.where(chosen, peak_part, -1e+30) for chosen, peak_part in zip(tier_masks, tier_peaks)]
    top_peak = functools.reduce(jnp.maximum, masked_peaks)
    numer = jnp.zeros((TOKENS, col_total), jnp.float32)
    denom = jnp.zeros((TOKENS, HEADS), jnp.float32)
    for chosen, peak_part, total_part, sum_part in zip(tier_masks, tier_peaks, tier_totals, tier_sums):
        factor = jnp.where(chosen, jnp.exp(jnp.where(chosen, peak_part, top_peak) - top_peak), 0.0)
        numer = numer + jnp.repeat(factor, HEAD_DIM, axis=1) * sum_part
        denom = denom + factor * total_part
    attended = (numer / jnp.repeat(denom, HEAD_DIM, axis=1)).astype(jnp.bfloat16)
    projected = jnp.dot(attended, out_proj, preferred_element_type=jnp.float32)
    resid = (states.astype(jnp.float32) + projected).astype(jnp.bfloat16)
    resid_wide = resid.astype(jnp.float32)
    row_mean = lax.optimization_barrier(jnp.mean(resid_wide, axis=1, keepdims=True))
    centered = resid_wide - row_mean
    row_var = lax.optimization_barrier(jnp.mean(centered * centered, axis=1, keepdims=True))
    normed = (centered * lax.rsqrt(row_var + 1e-05) * norm_gain[None, :]).astype(jnp.bfloat16)
    hidden = jax.nn.gelu(jnp.dot(normed, up_proj, preferred_element_type=jnp.float32), approximate=False).astype(jnp.bfloat16)
    mixed = jnp.dot(hidden, down_proj, preferred_element_type=jnp.float32)
    return (resid.astype(jnp.float32) + mixed).astype(jnp.bfloat16)
```

```python
import functools
import math

import jax
import jax.numpy as jnp
from jax import lax
from jax.experimental import pallas as pl
from jax.experimental.pallas import tpu as pltpu
from jax.sharding import PartitionSpec as P

HEAD_DIM = 80
SEG0 = 2048
SLAB = 256
ONES_AT = 3 * HEAD_DIM
CHUNK = 128
MASKED = -1e30
VMEM_BYTES = 48 * 1024 * 1024


def reversed_bits(value, bits):
    return sum((value >> b & 1) << (bits - 1 - b) for b in range(bits))


def slot_level(slot, tiers):
    return tiers - 1 - slot.bit_length()


def pack_kernel(tiers, q_ref, k_ref, v_ref, out_ref):
    stride = 2 ** (tiers - 1)
    rows = q_ref.shape[0]
    per = rows // stride
    place = lax.broadcasted_iota(jnp.int32, (rows, rows), 0)
    source = lax.broadcasted_iota(jnp.int32, (rows, rows), 1)
    wanted = (place & (per - 1)) * stride + (place >> (per.bit_length() - 1))
    perm = (wanted == source).astype(jnp.bfloat16)
    sorted_rows = [
        jnp.dot(perm, ref[...], preferred_element_type=jnp.float32) for ref in (v_ref, k_ref, q_ref)
    ]
    ones = jnp.ones((rows, SLAB - ONES_AT), jnp.float32)
    for head in range(out_ref.shape[0]):
        cols = slice(head * HEAD_DIM, (head + 1) * HEAD_DIM)
        slab = jnp.concatenate([part[:, cols] for part in sorted_rows] + [ones], axis=1).astype(
            jnp.bfloat16
        )
        for slot in range(stride):
            res = reversed_bits(slot, tiers - 1) ^ head % stride
            out_ref[head, slot] = slab[res * per : (res + 1) * per]


def attend_kernel(tiers, heads_dev, group, info_ref, x_ref, *rest):
    extra_refs, (out_ref, acc, peak) = rest[: tiers - 1], rest[tiers - 1 :]
    stride = 2 ** (tiers - 1)
    span = x_ref.shape[2]
    seq_pos = info_ref[0]
    plane = seq_pos // group
    head_class = (seq_pos % group * heads_dev + pl.program_id(0)) % stride
    scale = HEAD_DIM ** (-0.5) * math.log2(math.e)

    sel_row = lax.broadcasted_iota(jnp.int32, (SLAB, SLAB), 0)
    sel_col = lax.broadcasted_iota(jnp.int32, (SLAB, SLAB), 1)
    to_keys = ((sel_row == sel_col + HEAD_DIM) & (sel_row >= 2 * HEAD_DIM) & (sel_row < ONES_AT)).astype(
        jnp.bfloat16
    )

    def queries(rows):
        return jnp.dot(rows, to_keys, preferred_element_type=jnp.float32).astype(jnp.bfloat16)

    def score(q, keys):
        return lax.dot_general(q, keys, (((1,), (1,)), ((), ())), preferred_element_type=jnp.float32)

    tile = stride * CHUNK
    row_ids = lax.broadcasted_iota(jnp.int32, (tile, 1), 0)
    row_slot = row_ids // CHUNK
    row_pos = row_ids % CHUNK
    row_res = jnp.zeros_like(row_ids)
    row_level = jnp.zeros_like(row_ids)
    for slot in range(stride):
        row_res = jnp.where(row_slot == slot, reversed_bits(slot, tiers - 1) ^ head_class, row_res)
        row_level = jnp.where(row_slot == slot, slot_level(slot, tiers), row_level)
    row_bias = []
    for level in range(tiers):
        count = jnp.minimum(row_level, level) + 1
        bias = jnp.zeros((tile, 1), jnp.float32)
        for times in range(2, tiers + 1):
            bias = jnp.where(count == times, math.log2(times), bias)
        row_bias.append(bias)
    key_pos = lax.broadcasted_iota(jnp.int32, (tile, CHUNK), 1)

    for chunk in range(span // CHUNK):
        lo, hi = chunk * CHUNK, (chunk + 1) * CHUNK
        q = queries(jnp.concatenate([x_ref[0, slot, lo:hi] for slot in range(stride)], axis=0))
        scores = []
        for slot in range(stride):
            key_res = reversed_bits(slot, tiers - 1) ^ head_class
            last = row_pos - (key_res > row_res).astype(jnp.int32)
            part = score(q, x_ref[0, slot, lo:hi])
            scores.append((slot, lo, hi, jnp.where(key_pos <= last, part, MASKED)))
            if lo:
                scores.append((slot, 0, lo, score(q, x_ref[0, slot, 0:lo])))
        top = functools.reduce(
            jnp.maximum, [jnp.max(part, axis=1, keepdims=True) for _, _, _, part in scores]
        )
        total = jnp.zeros((tile, SLAB), jnp.float32)
        for slot, start, stop, part in scores:
            shift = top * scale - row_bias[slot_level(slot, tiers)]
            weight = jnp.exp2(part * scale - shift).astype(jnp.bfloat16)
            total = total + jnp.dot(
                weight, x_ref[0, slot, start:stop], preferred_element_type=jnp.float32
            )
        for slot in range(stride):
            rows = slice(slot * CHUNK, (slot + 1) * CHUNK)
            acc[slot, lo:hi] = total[rows]
            peak[slot, lo:hi] = jnp.broadcast_to(top[rows], (CHUNK, peak.shape[2]))

    for tier in range(1, tiers):
        extra = extra_refs[tier - 1]

        @pl.when(plane // 2 ** (tier - 1) % 2 == 1)
        def _():
            for q_slot in range(stride // 2**tier):
                q = queries(x_ref[0, q_slot])
                parts = [score(q, extra[0, slot]) for slot in range(extra.shape[1])]
                old = peak[q_slot][:, :1]
                top = functools.reduce(
                    jnp.maximum, [jnp.max(part, axis=1, keepdims=True) for part in parts], old
                )
                total = acc[q_slot] * jnp.exp2((old - top) * scale)
                for slot, part in enumerate(parts):
                    times = min(slot_level(q_slot, tiers), slot_level(slot, tiers)) - tier + 1
                    shift = top * scale - math.log2(times)
                    weight = jnp.exp2(part * scale - shift).astype(jnp.bfloat16)
                    total = total + jnp.dot(weight, extra[0, slot], preferred_element_type=jnp.float32)
                acc[q_slot] = total
                peak[q_slot] = jnp.broadcast_to(top, (span, peak.shape[2]))

    width = out_ref.shape[3]
    for slot in range(stride):
        total = acc[slot]
        out_ref[0, slot] = (total[:, :width] / total[:, ONES_AT : ONES_AT + 1]).astype(jnp.bfloat16)


def attention(query_rows, key_rows, value_rows):
    rows, cols = query_rows.shape
    heads = cols // HEAD_DIM
    seq_count = lax.axis_size("seq")
    seq_pos = lax.axis_index("seq")
    total_rows = rows * seq_count
    tiers = 0
    while SEG0 * 2**tiers <= total_rows and total_rows % (SEG0 * 2**tiers) == 0:
        tiers += 1
    stride = 2 ** (tiers - 1)
    per = rows // stride
    group = SEG0 // rows
    heads_dev = heads // group
    span = SEG0 // stride

    packed = pl.pallas_call(
        functools.partial(pack_kernel, tiers),
        out_shape=jax.ShapeDtypeStruct((heads, stride, per, SLAB), jnp.bfloat16),
        in_specs=[pl.BlockSpec(memory_space=pltpu.VMEM)] * 3,
        out_specs=pl.BlockSpec(memory_space=pltpu.VMEM),
        compiler_params=pltpu.CompilerParams(vmem_limit_bytes=VMEM_BYTES),
        name="pack_heads",
    )(query_rows, key_rows, value_rows)

    groups = [[base + i for i in range(group)] for base in range(0, seq_count, group)]
    swapped = lax.all_to_all(
        packed.reshape(group, heads_dev, stride, per, SLAB), "seq", 0, 0, axis_index_groups=groups
    )
    local = swapped.transpose(1, 2, 0, 3, 4).reshape(heads_dev, stride, span, SLAB)

    extras = []
    block = local[:, : stride // 2, None, :, : 2 * HEAD_DIM]
    for tier in range(1, tiers):
        step = group * 2 ** (tier - 1)
        up = [(i, i + step) for i in range(seq_count) if i // step % 2 == 0]
        down = [(i + step, i) for i, _ in up]
        slots = stride // 2**tier
        flat = block.transpose(0, 1, 2, 4, 3)
        got = lax.ppermute(flat, "seq", up).transpose(0, 1, 2, 4, 3)
        keys = got.reshape(heads_dev, slots, -1, 2 * HEAD_DIM)
        filler = jnp.zeros(keys.shape[:3] + (HEAD_DIM,), jnp.bfloat16)
        ones = jnp.ones(keys.shape[:3] + (SLAB - ONES_AT,), jnp.bfloat16)
        extras.append(jnp.concatenate([keys, filler, ones], axis=-1))
        if tier + 1 < tiers:
            kept = slots // 2
            below = lax.ppermute(flat[:, :kept], "seq", down).transpose(0, 1, 2, 4, 3)
            upper = seq_pos // step % 2 == 1
            mine, other = block[:, :kept], jnp.where(upper, got[:, :kept], below)
            block = jnp.concatenate([mine, other], axis=2)

    out = pl.pallas_call(
        functools.partial(attend_kernel, tiers, heads_dev, group),
        grid=(heads_dev,),
        out_shape=jax.ShapeDtypeStruct((heads_dev, stride, span, 128), jnp.bfloat16),
        in_specs=[
            pl.BlockSpec(memory_space=pltpu.SMEM),
            pl.BlockSpec((1, stride, span, SLAB), lambda h: (h, 0, 0, 0)),
        ]
        + [pl.BlockSpec((1,) + extra.shape[1:], lambda h: (h, 0, 0, 0)) for extra in extras],
        out_specs=pl.BlockSpec((1, stride, span, 128), lambda h: (h, 0, 0, 0)),
        scratch_shapes=[
            pltpu.VMEM((stride, span, SLAB), jnp.float32),
            pltpu.VMEM((stride, span, 128), jnp.float32),
        ],
        compiler_params=pltpu.CompilerParams(vmem_limit_bytes=VMEM_BYTES),
        name="attend",
    )(seq_pos.reshape(1).astype(jnp.int32), local, *extras)

    back = out[..., :HEAD_DIM].reshape(heads_dev, stride, group, per, HEAD_DIM)
    back = back.transpose(2, 0, 1, 4, 3)
    home = lax.all_to_all(back, "seq", 0, 0, axis_index_groups=groups)
    home = home.reshape(heads, stride, HEAD_DIM, per)
    ordered = []
    for head in range(heads):
        order = [reversed_bits(res ^ head % stride, tiers - 1) for res in range(stride)]
        ordered.append(jnp.stack([home[head, slot] for slot in order]))
    whole = jnp.stack(ordered)
    return whole.transpose(3, 1, 0, 2).reshape(rows, cols)


def per_device(states, query_rows, key_rows, value_rows, out_proj, norm_gain, up_proj, down_proj):
    model_width = states.shape[1]
    mp_pos = lax.axis_index("mp")
    down_whole = lax.all_gather(down_proj, "seq", axis=1, tiled=True)
    attended = attention(query_rows, key_rows, value_rows)
    projected = jnp.dot(attended, out_proj, preferred_element_type=jnp.float32)
    share = lax.psum_scatter(projected, "mp", scatter_dimension=1, tiled=True)
    half_width = share.shape[1]
    states_share = lax.dynamic_slice_in_dim(states, mp_pos * half_width, half_width, 1)
    resid_share = (states_share.astype(jnp.float32) + share).astype(jnp.bfloat16)
    share_wide = resid_share.astype(jnp.float32)
    part_sum, part_squares = lax.psum(
        (
            jnp.sum(share_wide, axis=1, keepdims=True),
            jnp.sum(share_wide * share_wide, axis=1, keepdims=True),
        ),
        "mp",
    )
    row_mean = part_sum / model_width
    row_var = part_squares / model_width - row_mean * row_mean
    gain_share = lax.dynamic_slice_in_dim(norm_gain, mp_pos * half_width, half_width, 0)
    normed_share = (
        (share_wide - row_mean) * lax.rsqrt(row_var + 1e-05) * gain_share[None, :]
    ).astype(jnp.bfloat16)
    normed = lax.all_gather(normed_share, "mp", axis=1, tiled=True)
    hidden = jax.nn.gelu(
        jnp.dot(normed, up_proj, preferred_element_type=jnp.float32), approximate=False
    ).astype(jnp.bfloat16)
    terms = jnp.dot(hidden, down_whole, preferred_element_type=jnp.float32)
    ffn_part = lax.psum_scatter(
        terms.astype(jnp.bfloat16), "mp", scatter_dimension=1, tiled=True
    ).astype(jnp.float32)
    return (resid_share.astype(jnp.float32) + ffn_part).astype(jnp.bfloat16)


def solution(mesh):
    in_specs = (
        P("seq", None),
        P("seq", "mp"),
        P("seq", "mp"),
        P("seq", "mp"),
        P("mp", None),
        P(),
        P(None, "mp"),
        P("mp", "seq"),
    )
    out_specs = P("seq", "mp")
    return jax.shard_map(
        per_device, mesh=mesh, in_specs=in_specs, out_specs=out_specs, check_vma=False
    )
```

```python
import functools
import math

import jax
import jax.numpy as jnp
from jax import lax
from jax.experimental import pallas as pl
from jax.experimental.pallas import tpu as pltpu
from jax.sharding import PartitionSpec as P

HEAD_DIM = 80
SEG0 = 2048
SLAB = 256
ONES_AT = 3 * HEAD_DIM
CHUNK = 128
MASKED = -1e30
VMEM_BYTES = 48 * 1024 * 1024


def reversed_bits(value, bits):
    return sum((value >> b & 1) << (bits - 1 - b) for b in range(bits))


def slot_level(slot, tiers):
    return tiers - 1 - slot.bit_length()


def pack_kernel(tiers, q_ref, k_ref, v_ref, out_ref):
    stride = 2 ** (tiers - 1)
    rows = q_ref.shape[0]
    per = rows // stride
    place = lax.broadcasted_iota(jnp.int32, (rows, rows), 0)
    source = lax.broadcasted_iota(jnp.int32, (rows, rows), 1)
    wanted = (place & (per - 1)) * stride + (place >> (per.bit_length() - 1))
    perm = (wanted == source).astype(jnp.bfloat16)
    sorted_rows = [
        jnp.dot(perm, ref[...], preferred_element_type=jnp.float32) for ref in (v_ref, k_ref, q_ref)
    ]
    ones = jnp.ones((rows, SLAB - ONES_AT), jnp.float32)
    for head in range(out_ref.shape[0]):
        cols = slice(head * HEAD_DIM, (head + 1) * HEAD_DIM)
        slab = jnp.concatenate([part[:, cols] for part in sorted_rows] + [ones], axis=1).astype(
            jnp.bfloat16
        )
        for slot in range(stride):
            res = reversed_bits(slot, tiers - 1) ^ head % stride
            out_ref[head, slot] = slab[res * per : (res + 1) * per]


def attend_kernel(tiers, heads_dev, group, info_ref, x_ref, *rest):
    extra_refs, (out_ref, acc, peak) = rest[: tiers - 1], rest[tiers - 1 :]
    stride = 2 ** (tiers - 1)
    span = x_ref.shape[2]
    seq_pos = info_ref[0]
    plane = seq_pos // group
    head_class = (seq_pos % group * heads_dev + pl.program_id(0)) % stride
    scale = HEAD_DIM ** (-0.5) * math.log2(math.e)

    sel_row = lax.broadcasted_iota(jnp.int32, (SLAB, SLAB), 0)
    sel_col = lax.broadcasted_iota(jnp.int32, (SLAB, SLAB), 1)
    to_keys = ((sel_row == sel_col + HEAD_DIM) & (sel_row >= 2 * HEAD_DIM) & (sel_row < ONES_AT)).astype(
        jnp.bfloat16
    )

    def queries(rows):
        return jnp.dot(rows, to_keys, preferred_element_type=jnp.float32).astype(jnp.bfloat16)

    def score(q, keys):
        return lax.dot_general(q, keys, (((1,), (1,)), ((), ())), preferred_element_type=jnp.float32)

    tile = stride * CHUNK
    row_ids = lax.broadcasted_iota(jnp.int32, (tile, 1), 0)
    row_slot = row_ids // CHUNK
    row_pos = row_ids % CHUNK
    row_res = jnp.zeros_like(row_ids)
    row_level = jnp.zeros_like(row_ids)
    for slot in range(stride):
        row_res = jnp.where(row_slot == slot, reversed_bits(slot, tiers - 1) ^ head_class, row_res)
        row_level = jnp.where(row_slot == slot, slot_level(slot, tiers), row_level)
    row_bias = []
    for level in range(tiers):
        count = jnp.minimum(row_level, level) + 1
        bias = jnp.zeros((tile, 1), jnp.float32)
        for times in range(2, tiers + 1):
            bias = jnp.where(count == times, math.log2(times), bias)
        row_bias.append(bias)
    key_pos = lax.broadcasted_iota(jnp.int32, (tile, CHUNK), 1)

    for chunk in range(span // CHUNK):
        lo, hi = chunk * CHUNK, (chunk + 1) * CHUNK
        q = queries(jnp.concatenate([x_ref[0, slot, lo:hi] for slot in range(stride)], axis=0))
        scores = []
        for slot in range(stride):
            key_res = reversed_bits(slot, tiers - 1) ^ head_class
            last = row_pos - (key_res > row_res).astype(jnp.int32)
            part = score(q, x_ref[0, slot, lo:hi])
            scores.append((slot, lo, hi, jnp.where(key_pos <= last, part, MASKED)))
            if lo:
                scores.append((slot, 0, lo, score(q, x_ref[0, slot, 0:lo])))
        top = functools.reduce(
            jnp.maximum, [jnp.max(part, axis=1, keepdims=True) for _, _, _, part in scores]
        )
        total = jnp.zeros((tile, SLAB), jnp.float32)
        for slot, start, stop, part in scores:
            shift = top * scale - row_bias[slot_level(slot, tiers)]
            weight = jnp.exp2(part * scale - shift).astype(jnp.bfloat16)
            total = total + jnp.dot(
                weight, x_ref[0, slot, start:stop], preferred_element_type=jnp.float32
            )
        for slot in range(stride):
            rows = slice(slot * CHUNK, (slot + 1) * CHUNK)
            acc[slot, lo:hi] = total[rows]
            peak[slot, lo:hi] = jnp.broadcast_to(top[rows], (CHUNK, peak.shape[2]))

    for tier in range(1, tiers):
        extra = extra_refs[tier - 1]

        @pl.when(plane // 2 ** (tier - 1) % 2 == 1)
        def _():
            for q_slot in range(stride // 2**tier):
                q = queries(x_ref[0, q_slot])
                parts = [score(q, extra[0, slot]) for slot in range(extra.shape[1])]
                old = peak[q_slot][:, :1]
                top = functools.reduce(
                    jnp.maximum, [jnp.max(part, axis=1, keepdims=True) for part in parts], old
                )
                total = acc[q_slot] * jnp.exp2((old - top) * scale)
                for slot, part in enumerate(parts):
                    times = min(slot_level(q_slot, tiers), slot_level(slot, tiers)) - tier + 1
                    shift = top * scale - math.log2(times)
                    weight = jnp.exp2(part * scale - shift).astype(jnp.bfloat16)
                    total = total + jnp.dot(weight, extra[0, slot], preferred_element_type=jnp.float32)
                acc[q_slot] = total
                peak[q_slot] = jnp.broadcast_to(top, (span, peak.shape[2]))

    width = out_ref.shape[3]
    for slot in range(stride):
        total = acc[slot]
        out_ref[0, slot] = (total[:, :width] / total[:, ONES_AT : ONES_AT + 1]).astype(jnp.bfloat16)


def attention(query_rows, key_rows, value_rows):
    rows, cols = query_rows.shape
    heads = cols // HEAD_DIM
    seq_count = lax.axis_size("seq")
    seq_pos = lax.axis_index("seq")
    total_rows = rows * seq_count
    tiers = 0
    while SEG0 * 2**tiers <= total_rows and total_rows % (SEG0 * 2**tiers) == 0:
        tiers += 1
    stride = 2 ** (tiers - 1)
    per = rows // stride
    group = SEG0 // rows
    heads_dev = heads // group
    span = SEG0 // stride

    packed = pl.pallas_call(
        functools.partial(pack_kernel, tiers),
        out_shape=jax.ShapeDtypeStruct((heads, stride, per, SLAB), jnp.bfloat16),
        in_specs=[pl.BlockSpec(memory_space=pltpu.VMEM)] * 3,
        out_specs=pl.BlockSpec(memory_space=pltpu.VMEM),
        compiler_params=pltpu.CompilerParams(vmem_limit_bytes=VMEM_BYTES),
        name="pack_heads",
    )(query_rows, key_rows, value_rows)

    groups = [[base + i for i in range(group)] for base in range(0, seq_count, group)]
    swapped = lax.all_to_all(
        packed.reshape(group, heads_dev, stride, per, SLAB), "seq", 0, 0, axis_index_groups=groups
    )
    local = swapped.transpose(1, 2, 0, 3, 4).reshape(heads_dev, stride, span, SLAB)

    extras = []
    block = local[:, : stride // 2, None, :, : 2 * HEAD_DIM]
    for tier in range(1, tiers):
        step = group * 2 ** (tier - 1)
        up = [(i, i + step) for i in range(seq_count) if i // step % 2 == 0]
        down = [(i + step, i) for i, _ in up]
        slots = stride // 2**tier
        flat = block.transpose(0, 1, 2, 4, 3)
        got = lax.ppermute(flat, "seq", up).transpose(0, 1, 2, 4, 3)
        keys = got.reshape(heads_dev, slots, -1, 2 * HEAD_DIM)
        filler = jnp.zeros(keys.shape[:3] + (HEAD_DIM,), jnp.bfloat16)
        ones = jnp.ones(keys.shape[:3] + (SLAB - ONES_AT,), jnp.bfloat16)
        extras.append(jnp.concatenate([keys, filler, ones], axis=-1))
        if tier + 1 < tiers:
            kept = slots // 2
            below = lax.ppermute(flat[:, :kept], "seq", down).transpose(0, 1, 2, 4, 3)
            upper = seq_pos // step % 2 == 1
            mine, other = block[:, :kept], jnp.where(upper, got[:, :kept], below)
            block = jnp.concatenate([mine, other], axis=2)

    out = pl.pallas_call(
        functools.partial(attend_kernel, tiers, heads_dev, group),
        grid=(heads_dev,),
        out_shape=jax.ShapeDtypeStruct((heads_dev, stride, span, 128), jnp.bfloat16),
        in_specs=[
            pl.BlockSpec(memory_space=pltpu.SMEM),
            pl.BlockSpec((1, stride, span, SLAB), lambda h: (h, 0, 0, 0)),
        ]
        + [pl.BlockSpec((1,) + extra.shape[1:], lambda h: (h, 0, 0, 0)) for extra in extras],
        out_specs=pl.BlockSpec((1, stride, span, 128), lambda h: (h, 0, 0, 0)),
        scratch_shapes=[
            pltpu.VMEM((stride, span, SLAB), jnp.float32),
            pltpu.VMEM((stride, span, 128), jnp.float32),
        ],
        compiler_params=pltpu.CompilerParams(vmem_limit_bytes=VMEM_BYTES),
        name="attend",
    )(seq_pos.reshape(1).astype(jnp.int32), local, *extras)

    back = out[..., :HEAD_DIM].reshape(heads_dev, stride, group, per, HEAD_DIM)
    back = back.transpose(2, 0, 1, 4, 3)
    home = lax.all_to_all(back, "seq", 0, 0, axis_index_groups=groups)
    home = home.reshape(heads, stride, HEAD_DIM, per)
    ordered = []
    for head in range(heads):
        order = [reversed_bits(res ^ head % stride, tiers - 1) for res in range(stride)]
        ordered.append(jnp.stack([home[head, slot] for slot in order]))
    whole = jnp.stack(ordered)
    return whole.transpose(3, 1, 0, 2).reshape(rows, cols)


def lift_kernel(att_ref, states_ref, proj_ref, gain_ref, up_ref, resid_ref, hidden_ref, normed):
    @pl.when(pl.program_id(0) == 0)
    def _():
        projected = jnp.dot(att_ref[...], proj_ref[...], preferred_element_type=jnp.float32)
        resid = (states_ref[...].astype(jnp.float32) + projected).astype(jnp.bfloat16)
        resid_ref[...] = resid
        wide = resid.astype(jnp.float32)
        centered = wide - jnp.mean(wide, axis=1, keepdims=True)
        var = jnp.mean(centered * centered, axis=1, keepdims=True)
        normed[...] = (centered * lax.rsqrt(var + 1e-05) * gain_ref[...]).astype(jnp.bfloat16)

    raw = jnp.dot(normed[...], up_ref[...], preferred_element_type=jnp.float32)
    hidden_ref[...] = (0.5 * raw * (1.0 + lax.erf(raw * math.sqrt(0.5)))).astype(jnp.bfloat16)


def lower_kernel(hidden_ref, down_ref, resid_ref, out_ref):
    mixed = lax.dot_general(
        hidden_ref[...],
        down_ref[...],
        (((1,), (1,)), ((), ())),
        preferred_element_type=jnp.float32,
    )
    out_ref[...] = (resid_ref[...].astype(jnp.float32) + mixed).astype(jnp.bfloat16)


def feed_forward(attended, states, out_proj, norm_gain, up_proj, down_rows):
    rows, width = states.shape
    units = up_proj.shape[1]
    step = math.gcd(units, 512)
    whole = lambda i: (0, 0)
    resid, hidden = pl.pallas_call(
        lift_kernel,
        grid=(units // step,),
        out_shape=(
            jax.ShapeDtypeStruct((rows, width), jnp.bfloat16),
            jax.ShapeDtypeStruct((rows, units), jnp.bfloat16),
        ),
        in_specs=[
            pl.BlockSpec(attended.shape, whole),
            pl.BlockSpec((rows, width), whole),
            pl.BlockSpec(out_proj.shape, whole),
            pl.BlockSpec((1, width), whole),
            pl.BlockSpec((width, step), lambda i: (0, i)),
        ],
        out_specs=(
            pl.BlockSpec((rows, width), whole),
            pl.BlockSpec((rows, step), lambda i: (0, i)),
        ),
        scratch_shapes=[pltpu.VMEM((rows, width), jnp.bfloat16)],
        compiler_params=pltpu.CompilerParams(vmem_limit_bytes=VMEM_BYTES),
        cost_estimate=pl.CostEstimate(
            flops=2 * rows * width * (units + attended.shape[1]),
            bytes_accessed=2 * width * (units + attended.shape[1]),
            transcendentals=rows * units,
        ),
        name="project_and_lift",
    )(attended, states, out_proj, norm_gain.reshape(1, width), up_proj)
    part = math.gcd(width, 256)
    return pl.pallas_call(
        lower_kernel,
        grid=(width // part,),
        out_shape=jax.ShapeDtypeStruct((rows, width), jnp.bfloat16),
        in_specs=[
            pl.BlockSpec((rows, units), whole),
            pl.BlockSpec((part, units), lambda i: (i, 0)),
            pl.BlockSpec((rows, part), lambda i: (0, i)),
        ],
        out_specs=pl.BlockSpec((rows, part), lambda i: (0, i)),
        compiler_params=pltpu.CompilerParams(vmem_limit_bytes=VMEM_BYTES),
        name="lower",
    )(hidden, down_rows, resid)


def per_device(states, query_rows, key_rows, value_rows, out_proj, norm_gain, up_proj, down_proj):
    model_width = states.shape[1]
    mp_pos = lax.axis_index("mp")
    down_rows = lax.all_gather(down_proj.T, "seq", axis=0, tiled=True)
    attended = attention(query_rows, key_rows, value_rows)
    if lax.axis_size("mp") == 1:
        return feed_forward(attended, states, out_proj, norm_gain, up_proj, down_rows)
    projected = jnp.dot(attended, out_proj, preferred_element_type=jnp.float32)
    share = lax.psum_scatter(projected, "mp", scatter_dimension=1, tiled=True)
    half_width = share.shape[1]
    states_share = lax.dynamic_slice_in_dim(states, mp_pos * half_width, half_width, 1)
    resid_share = (states_share.astype(jnp.float32) + share).astype(jnp.bfloat16)
    share_wide = resid_share.astype(jnp.float32)
    part_sum, part_squares = lax.psum(
        (
            jnp.sum(share_wide, axis=1, keepdims=True),
            jnp.sum(share_wide * share_wide, axis=1, keepdims=True),
        ),
        "mp",
    )
    row_mean = part_sum / model_width
    row_var = part_squares / model_width - row_mean * row_mean
    gain_share = lax.dynamic_slice_in_dim(norm_gain, mp_pos * half_width, half_width, 0)
    normed_share = (
        (share_wide - row_mean) * lax.rsqrt(row_var + 1e-05) * gain_share[None, :]
    ).astype(jnp.bfloat16)
    normed = lax.all_gather(normed_share, "mp", axis=1, tiled=True)
    hidden = jax.nn.gelu(
        jnp.dot(normed, up_proj, preferred_element_type=jnp.float32), approximate=False
    ).astype(jnp.bfloat16)
    terms = lax.dot_general(
        hidden, down_rows, (((1,), (1,)), ((), ())), preferred_element_type=jnp.float32
    )
    ffn_part = lax.psum_scatter(
        terms.astype(jnp.bfloat16), "mp", scatter_dimension=1, tiled=True
    ).astype(jnp.float32)
    return (resid_share.astype(jnp.float32) + ffn_part).astype(jnp.bfloat16)


def solution(mesh):
    in_specs = (
        P("seq", None),
        P("seq", "mp"),
        P("seq", "mp"),
        P("seq", "mp"),
        P("mp", None),
        P(),
        P(None, "mp"),
        P("mp", "seq"),
    )
    out_specs = P("seq", "mp")
    return jax.shard_map(
        per_device, mesh=mesh, in_specs=in_specs, out_specs=out_specs, check_vma=False
    )
```

```python
import functools
import math

import jax
import jax.numpy as jnp
from jax import lax
from jax.experimental import pallas as pl
from jax.experimental.pallas import tpu as pltpu
from jax.sharding import PartitionSpec as P

HEAD_DIM = 80
SEG0 = 2048
SLAB = 256
ONES_AT = 3 * HEAD_DIM
CHUNK = 128
MASKED = -1e30
VMEM_BYTES = 48 * 1024 * 1024


def reversed_bits(value, bits):
    return sum((value >> b & 1) << (bits - 1 - b) for b in range(bits))


def slot_level(slot, tiers):
    return tiers - 1 - slot.bit_length()


def pack_kernel(tiers, q_ref, k_ref, v_ref, out_ref):
    stride = 2 ** (tiers - 1)
    rows = q_ref.shape[0]
    per = rows // stride
    place = lax.broadcasted_iota(jnp.int32, (rows, rows), 0)
    source = lax.broadcasted_iota(jnp.int32, (rows, rows), 1)
    wanted = (place & (per - 1)) * stride + (place >> (per.bit_length() - 1))
    perm = (wanted == source).astype(jnp.bfloat16)
    sorted_rows = [
        jnp.dot(perm, ref[...], preferred_element_type=jnp.float32) for ref in (v_ref, k_ref, q_ref)
    ]
    ones = jnp.ones((rows, SLAB - ONES_AT), jnp.float32)
    for head in range(out_ref.shape[0]):
        cols = slice(head * HEAD_DIM, (head + 1) * HEAD_DIM)
        slab = jnp.concatenate([part[:, cols] for part in sorted_rows] + [ones], axis=1).astype(
            jnp.bfloat16
        )
        for slot in range(stride):
            res = reversed_bits(slot, tiers - 1) ^ head % stride
            out_ref[head, slot] = slab[res * per : (res + 1) * per]


def query_part(rows):
    sel_row = lax.broadcasted_iota(jnp.int32, (SLAB, SLAB), 0)
    sel_col = lax.broadcasted_iota(jnp.int32, (SLAB, SLAB), 1)
    to_keys = ((sel_row == sel_col + HEAD_DIM) & (sel_row >= 2 * HEAD_DIM) & (sel_row < ONES_AT)).astype(
        jnp.bfloat16
    )
    return jnp.dot(rows, to_keys, preferred_element_type=jnp.float32).astype(jnp.bfloat16)


def segment_kernel(tiers, heads_dev, group, info_ref, x_ref, out_ref, acc_ref, peak_ref):
    stride = 2 ** (tiers - 1)
    span = x_ref.shape[2]
    seq_pos = info_ref[0]
    head_class = (seq_pos % group * heads_dev + pl.program_id(0)) % stride
    scale = HEAD_DIM ** (-0.5) * math.log2(math.e)

    def score(q, keys):
        return lax.dot_general(q, keys, (((1,), (1,)), ((), ())), preferred_element_type=jnp.float32)

    tile = stride * CHUNK
    row_ids = lax.broadcasted_iota(jnp.int32, (tile, 1), 0)
    row_slot = row_ids // CHUNK
    row_pos = row_ids % CHUNK
    row_res = jnp.zeros_like(row_ids)
    row_level = jnp.zeros_like(row_ids)
    for slot in range(stride):
        row_res = jnp.where(row_slot == slot, reversed_bits(slot, tiers - 1) ^ head_class, row_res)
        row_level = jnp.where(row_slot == slot, slot_level(slot, tiers), row_level)
    row_bias = []
    for level in range(tiers):
        count = jnp.minimum(row_level, level) + 1
        bias = jnp.zeros((tile, 1), jnp.float32)
        for times in range(2, tiers + 1):
            bias = jnp.where(count == times, math.log2(times), bias)
        row_bias.append(bias)
    key_pos = lax.broadcasted_iota(jnp.int32, (tile, CHUNK), 1)

    for chunk in range(span // CHUNK):
        lo, hi = chunk * CHUNK, (chunk + 1) * CHUNK
        q = query_part(jnp.concatenate([x_ref[0, slot, lo:hi] for slot in range(stride)], axis=0))
        scores = []
        for slot in range(stride):
            key_res = reversed_bits(slot, tiers - 1) ^ head_class
            last = row_pos - (key_res > row_res).astype(jnp.int32)
            part = score(q, x_ref[0, slot, lo:hi])
            scores.append((slot, lo, hi, jnp.where(key_pos <= last, part, MASKED)))
            if lo:
                scores.append((slot, 0, lo, score(q, x_ref[0, slot, 0:lo])))
        top = functools.reduce(
            jnp.maximum, [jnp.max(part, axis=1, keepdims=True) for _, _, _, part in scores]
        )
        total = jnp.zeros((tile, SLAB), jnp.float32)
        for slot, start, stop, part in scores:
            shift = top * scale - row_bias[slot_level(slot, tiers)]
            weight = jnp.exp2(part * scale - shift).astype(jnp.bfloat16)
            total = total + jnp.dot(
                weight, x_ref[0, slot, start:stop], preferred_element_type=jnp.float32
            )
        width = out_ref.shape[3]
        for slot in range(stride):
            rows = slice(slot * CHUNK, (slot + 1) * CHUNK)
            if slot < stride // 2:
                acc_ref[0, slot, lo:hi] = total[rows]
                peak_ref[0, slot, lo:hi] = jnp.broadcast_to(top[rows], (CHUNK, peak_ref.shape[3]))
            else:
                done = total[rows, :width] / total[rows, ONES_AT : ONES_AT + 1]
                out_ref[0, slot - stride // 2, lo:hi] = done.astype(jnp.bfloat16)


def earlier_kernel(tiers, group, info_ref, x_ref, acc_in, peak_in, *rest):
    extra_refs, (out_ref, acc, peak) = rest[:-3], rest[-3:]
    half, span = x_ref.shape[1:3]
    stride = 2 * half
    plane = info_ref[0] // group
    scale = HEAD_DIM ** (-0.5) * math.log2(math.e)
    depth = 2 * HEAD_DIM
    acc[...] = acc_in[0]
    peak[...] = peak_in[0]
    at = 0
    for tier in range(1, tiers):
        extras = extra_refs[at : at + 2 ** (tier - 1)]
        at += 2 ** (tier - 1)

        @pl.when(plane // 2 ** (tier - 1) % 2 == 1)
        def _():
            for q_slot in range(stride // 2**tier):
                q = query_part(x_ref[0, q_slot])[:, :depth]
                parts = [
                    (slot, ref, jnp.dot(q, ref[0, slot], preferred_element_type=jnp.float32))
                    for ref in extras
                    for slot in range(ref.shape[1])
                ]
                old = peak[q_slot][:, :1]
                top = functools.reduce(
                    jnp.maximum, [jnp.max(part, axis=1, keepdims=True) for _, _, part in parts], old
                )
                keep = jnp.exp2((old - top) * scale)
                numer = acc[q_slot, :, :128] * keep
                denom = acc[q_slot, :, ONES_AT : ONES_AT + 1] * keep
                for slot, ref, part in parts:
                    times = min(slot_level(q_slot, tiers), slot_level(slot, tiers)) - tier + 1
                    weight = jnp.exp2(part * scale - (top * scale - math.log2(times)))
                    denom = denom + jnp.sum(weight, axis=1, keepdims=True)
                    numer = (
                        numer
                        + lax.dot_general(
                            weight.astype(jnp.bfloat16),
                            ref[0, slot],
                            (((1,), (1,)), ((), ())),
                            preferred_element_type=jnp.float32,
                        )[:, :128]
                    )
                acc[q_slot, :, :128] = numer
                acc[q_slot, :, 128:] = jnp.broadcast_to(denom, (span, SLAB - 128))
                peak[q_slot] = jnp.broadcast_to(top, (span, peak.shape[2]))

    for slot in range(half):
        done = acc[slot, :, :128] / acc[slot, :, ONES_AT : ONES_AT + 1]
        out_ref[0, slot] = done.astype(jnp.bfloat16)


def attention(query_rows, key_rows, value_rows):
    rows, cols = query_rows.shape
    heads = cols // HEAD_DIM
    seq_count = lax.axis_size("seq")
    seq_pos = lax.axis_index("seq")
    total_rows = rows * seq_count
    tiers = 0
    while SEG0 * 2**tiers <= total_rows and total_rows % (SEG0 * 2**tiers) == 0:
        tiers += 1
    stride = 2 ** (tiers - 1)
    per = rows // stride
    group = SEG0 // rows
    heads_dev = heads // group
    span = SEG0 // stride

    packed = pl.pallas_call(
        functools.partial(pack_kernel, tiers),
        out_shape=jax.ShapeDtypeStruct((heads, stride, per, SLAB), jnp.bfloat16),
        in_specs=[pl.BlockSpec(memory_space=pltpu.VMEM)] * 3,
        out_specs=pl.BlockSpec(memory_space=pltpu.VMEM),
        compiler_params=pltpu.CompilerParams(vmem_limit_bytes=VMEM_BYTES),
        name="pack_heads",
    )(query_rows, key_rows, value_rows)

    groups = [[base + i for i in range(group)] for base in range(0, seq_count, group)]
    swapped = lax.all_to_all(
        packed.reshape(group, heads_dev, stride, per, SLAB), "seq", 0, 0, axis_index_groups=groups
    )
    local = swapped.transpose(1, 2, 0, 3, 4).reshape(heads_dev, stride, span, SLAB)

    half = stride // 2
    flat = local[:, :half, :, : 2 * HEAD_DIM].transpose(0, 1, 3, 2)
    extras = []
    for tier in range(1, tiers):
        bit = 2 ** (tier - 1)
        for twist in range(bit):
            pairs = [
                (i, ((i // group | bit) ^ twist) * group + i % group)
                for i in range(seq_count)
                if i // group & bit == 0
            ]
            extras.append(lax.ppermute(flat[:, : stride // 2**tier], "seq", pairs))

    info = seq_pos.reshape(1).astype(jnp.int32)
    smem = pl.BlockSpec(memory_space=pltpu.SMEM)

    def per_head(shape):
        return pl.BlockSpec((1,) + tuple(shape[1:]), lambda h: (h,) + (0,) * (len(shape) - 1))

    upper_shape = (heads_dev, stride - half, span, 128)
    acc_shape = (heads_dev, half, span, SLAB)
    peak_shape = (heads_dev, half, span, 128)
    upper, acc, peak = pl.pallas_call(
        functools.partial(segment_kernel, tiers, heads_dev, group),
        grid=(heads_dev,),
        out_shape=(
            jax.ShapeDtypeStruct(upper_shape, jnp.bfloat16),
            jax.ShapeDtypeStruct(acc_shape, jnp.float32),
            jax.ShapeDtypeStruct(peak_shape, jnp.float32),
        ),
        in_specs=[smem, per_head(local.shape)],
        out_specs=(per_head(upper_shape), per_head(acc_shape), per_head(peak_shape)),
        compiler_params=pltpu.CompilerParams(vmem_limit_bytes=VMEM_BYTES),
        cost_estimate=pl.CostEstimate(
            flops=heads_dev * SEG0 * SEG0 * 4 * SLAB,
            bytes_accessed=heads_dev * SEG0 * SLAB * 6,
            transcendentals=heads_dev * SEG0 * SEG0,
        ),
        name="segment_attend",
    )(info, local)

    groups = [[base + i for i in range(group)] for base in range(0, seq_count, group)]

    def send_home(part):
        part = part[..., :HEAD_DIM].reshape(heads_dev, -1, group, per, HEAD_DIM)
        part = part.transpose(2, 0, 1, 4, 3)
        part = lax.all_to_all(part, "seq", 0, 0, axis_index_groups=groups)
        return part.reshape(heads, -1, HEAD_DIM, per)

    upper_home = send_home(upper)
    lower = pl.pallas_call(
        functools.partial(earlier_kernel, tiers, group),
        grid=(heads_dev,),
        out_shape=jax.ShapeDtypeStruct(peak_shape, jnp.bfloat16),
        in_specs=[smem, pl.BlockSpec((1, half, span, SLAB), lambda h: (h, 0, 0, 0))]
        + [per_head(acc_shape), per_head(peak_shape)]
        + [per_head(extra.shape) for extra in extras],
        out_specs=per_head(peak_shape),
        scratch_shapes=[
            pltpu.VMEM((half, span, SLAB), jnp.float32),
            pltpu.VMEM((half, span, 128), jnp.float32),
        ],
        compiler_params=pltpu.CompilerParams(vmem_limit_bytes=VMEM_BYTES),
        name="earlier_segments",
    )(info, local, acc, peak, *extras)
    home = jnp.concatenate([send_home(lower), upper_home], axis=1)
    ordered = []
    for head in range(heads):
        order = [reversed_bits(res ^ head % stride, tiers - 1) for res in range(stride)]
        ordered.append(jnp.stack([home[head, slot] for slot in order]))
    whole = jnp.stack(ordered)
    return whole.transpose(3, 1, 0, 2).reshape(rows, cols)


def lift_kernel(att_ref, states_ref, proj_ref, gain_ref, up_ref, resid_ref, hidden_ref, normed):
    @pl.when(pl.program_id(0) == 0)
    def _():
        projected = jnp.dot(att_ref[...], proj_ref[...], preferred_element_type=jnp.float32)
        resid = (states_ref[...].astype(jnp.float32) + projected).astype(jnp.bfloat16)
        resid_ref[...] = resid
        wide = resid.astype(jnp.float32)
        centered = wide - jnp.mean(wide, axis=1, keepdims=True)
        var = jnp.mean(centered * centered, axis=1, keepdims=True)
        normed[...] = (centered * lax.rsqrt(var + 1e-05) * gain_ref[...]).astype(jnp.bfloat16)

    raw = jnp.dot(normed[...], up_ref[...], preferred_element_type=jnp.float32)
    hidden_ref[...] = (0.5 * raw * (1.0 + lax.erf(raw * math.sqrt(0.5)))).astype(jnp.bfloat16)


def lower_kernel(hidden_ref, down_ref, resid_ref, out_ref):
    mixed = lax.dot_general(
        hidden_ref[...],
        down_ref[...],
        (((1,), (1,)), ((), ())),
        preferred_element_type=jnp.float32,
    )
    out_ref[...] = (resid_ref[...].astype(jnp.float32) + mixed).astype(jnp.bfloat16)


def feed_forward(attended, states, out_proj, norm_gain, up_proj, down_rows):
    rows, width = states.shape
    units = up_proj.shape[1]
    step = math.gcd(units, 512)
    whole = lambda i: (0, 0)
    resid, hidden = pl.pallas_call(
        lift_kernel,
        grid=(units // step,),
        out_shape=(
            jax.ShapeDtypeStruct((rows, width), jnp.bfloat16),
            jax.ShapeDtypeStruct((rows, units), jnp.bfloat16),
        ),
        in_specs=[
            pl.BlockSpec(attended.shape, whole),
            pl.BlockSpec((rows, width), whole),
            pl.BlockSpec(out_proj.shape, whole),
            pl.BlockSpec((1, width), whole),
            pl.BlockSpec((width, step), lambda i: (0, i)),
        ],
        out_specs=(
            pl.BlockSpec((rows, width), whole),
            pl.BlockSpec((rows, step), lambda i: (0, i)),
        ),
        scratch_shapes=[pltpu.VMEM((rows, width), jnp.bfloat16)],
        compiler_params=pltpu.CompilerParams(vmem_limit_bytes=VMEM_BYTES),
        cost_estimate=pl.CostEstimate(
            flops=2 * rows * width * (units + attended.shape[1]),
            bytes_accessed=2 * width * (units + attended.shape[1]),
            transcendentals=rows * units,
        ),
        name="project_and_lift",
    )(attended, states, out_proj, norm_gain.reshape(1, width), up_proj)
    part = math.gcd(width, 256)
    return pl.pallas_call(
        lower_kernel,
        grid=(width // part,),
        out_shape=jax.ShapeDtypeStruct((rows, width), jnp.bfloat16),
        in_specs=[
            pl.BlockSpec((rows, units), whole),
            pl.BlockSpec((part, units), lambda i: (i, 0)),
            pl.BlockSpec((rows, part), lambda i: (0, i)),
        ],
        out_specs=pl.BlockSpec((rows, part), lambda i: (0, i)),
        compiler_params=pltpu.CompilerParams(vmem_limit_bytes=VMEM_BYTES),
        name="lower",
    )(hidden, down_rows, resid)


def per_device(states, query_rows, key_rows, value_rows, out_proj, norm_gain, up_proj, down_proj):
    model_width = states.shape[1]
    mp_pos = lax.axis_index("mp")
    down_rows = lax.all_gather(down_proj.T, "seq", axis=0, tiled=True)
    attended = attention(query_rows, key_rows, value_rows)
    if lax.axis_size("mp") == 1:
        return feed_forward(attended, states, out_proj, norm_gain, up_proj, down_rows)
    projected = jnp.dot(attended, out_proj, preferred_element_type=jnp.float32)
    share = lax.psum_scatter(projected, "mp", scatter_dimension=1, tiled=True)
    half_width = share.shape[1]
    states_share = lax.dynamic_slice_in_dim(states, mp_pos * half_width, half_width, 1)
    resid_share = (states_share.astype(jnp.float32) + share).astype(jnp.bfloat16)
    share_wide = resid_share.astype(jnp.float32)
    part_sum, part_squares = lax.psum(
        (
            jnp.sum(share_wide, axis=1, keepdims=True),
            jnp.sum(share_wide * share_wide, axis=1, keepdims=True),
        ),
        "mp",
    )
    row_mean = part_sum / model_width
    row_var = part_squares / model_width - row_mean * row_mean
    gain_share = lax.dynamic_slice_in_dim(norm_gain, mp_pos * half_width, half_width, 0)
    normed_share = (
        (share_wide - row_mean) * lax.rsqrt(row_var + 1e-05) * gain_share[None, :]
    ).astype(jnp.bfloat16)
    normed = lax.all_gather(normed_share, "mp", axis=1, tiled=True)
    hidden = jax.nn.gelu(
        jnp.dot(normed, up_proj, preferred_element_type=jnp.float32), approximate=False
    ).astype(jnp.bfloat16)
    terms = lax.dot_general(
        hidden, down_rows, (((1,), (1,)), ((), ())), preferred_element_type=jnp.float32
    )
    ffn_part = lax.psum_scatter(
        terms.astype(jnp.bfloat16), "mp", scatter_dimension=1, tiled=True
    ).astype(jnp.float32)
    return (resid_share.astype(jnp.float32) + ffn_part).astype(jnp.bfloat16)


def solution(mesh):
    in_specs = (
        P("seq", None),
        P("seq", "mp"),
        P("seq", "mp"),
        P("seq", "mp"),
        P("mp", None),
        P(),
        P(None, "mp"),
        P("mp", "seq"),
    )
    out_specs = P("seq", "mp")
    return jax.shard_map(
        per_device, mesh=mesh, in_specs=in_specs, out_specs=out_specs, check_vma=False
    )
```

```python
import functools
import math

import jax
import jax.numpy as jnp
from jax import lax
from jax.experimental import pallas as pl
from jax.experimental.pallas import tpu as pltpu
from jax.sharding import PartitionSpec as P

HEAD_DIM = 80
SEG0 = 2048
SLAB = 256
ONES_AT = 3 * HEAD_DIM
CHUNK = 128
MASKED = -1e30
VMEM_BYTES = 30 * 1024 * 1024


def reversed_bits(value, bits):
    return sum((value >> b & 1) << (bits - 1 - b) for b in range(bits))


def slot_level(slot, tiers):
    return tiers - 1 - slot.bit_length()


def pack_kernel(tiers, q_ref, k_ref, v_ref, out_ref):
    stride = 2 ** (tiers - 1)
    rows = q_ref.shape[0]
    per = rows // stride
    place = lax.broadcasted_iota(jnp.int32, (rows, rows), 0)
    source = lax.broadcasted_iota(jnp.int32, (rows, rows), 1)
    wanted = (place & (per - 1)) * stride + (place >> (per.bit_length() - 1))
    perm = (wanted == source).astype(jnp.bfloat16)
    sorted_rows = [
        jnp.dot(perm, ref[...], preferred_element_type=jnp.float32) for ref in (v_ref, k_ref, q_ref)
    ]
    ones = jnp.ones((rows, SLAB - ONES_AT), jnp.float32)
    for head in range(out_ref.shape[0]):
        cols = slice(head * HEAD_DIM, (head + 1) * HEAD_DIM)
        slab = jnp.concatenate([part[:, cols] for part in sorted_rows] + [ones], axis=1).astype(
            jnp.bfloat16
        )
        for slot in range(stride):
            res = reversed_bits(slot, tiers - 1) ^ head % stride
            out_ref[head, slot] = slab[res * per : (res + 1) * per]


def query_part(rows):
    sel_row = lax.broadcasted_iota(jnp.int32, (SLAB, SLAB), 0)
    sel_col = lax.broadcasted_iota(jnp.int32, (SLAB, SLAB), 1)
    to_keys = ((sel_row == sel_col + HEAD_DIM) & (sel_row >= 2 * HEAD_DIM) & (sel_row < ONES_AT)).astype(
        jnp.bfloat16
    )
    return jnp.dot(rows, to_keys, preferred_element_type=jnp.float32).astype(jnp.bfloat16)


def segment_kernel(tiers, heads_dev, group, info_ref, x_ref, out_ref, acc_ref, peak_ref):
    stride = 2 ** (tiers - 1)
    span = x_ref.shape[2]
    seq_pos = info_ref[0]
    head_class = (seq_pos % group * heads_dev + pl.program_id(0)) % stride
    scale = HEAD_DIM ** (-0.5) * math.log2(math.e)

    def score(q, keys):
        return lax.dot_general(q, keys, (((1,), (1,)), ((), ())), preferred_element_type=jnp.float32)

    tile = stride * CHUNK
    row_ids = lax.broadcasted_iota(jnp.int32, (tile, 1), 0)
    row_slot = row_ids // CHUNK
    row_pos = row_ids % CHUNK
    row_res = jnp.zeros_like(row_ids)
    row_level = jnp.zeros_like(row_ids)
    for slot in range(stride):
        row_res = jnp.where(row_slot == slot, reversed_bits(slot, tiers - 1) ^ head_class, row_res)
        row_level = jnp.where(row_slot == slot, slot_level(slot, tiers), row_level)
    row_bias = []
    for level in range(tiers):
        count = jnp.minimum(row_level, level) + 1
        bias = jnp.zeros((tile, 1), jnp.float32)
        for times in range(2, tiers + 1):
            bias = jnp.where(count == times, math.log2(times), bias)
        row_bias.append(bias)
    key_pos = lax.broadcasted_iota(jnp.int32, (tile, CHUNK), 1)

    for chunk in range(span // CHUNK):
        lo, hi = chunk * CHUNK, (chunk + 1) * CHUNK
        q = query_part(jnp.concatenate([x_ref[0, slot, lo:hi] for slot in range(stride)], axis=0))
        scores = []
        for slot in range(stride):
            key_res = reversed_bits(slot, tiers - 1) ^ head_class
            last = row_pos - (key_res > row_res).astype(jnp.int32)
            part = score(q, x_ref[0, slot, lo:hi])
            scores.append((slot, lo, hi, jnp.where(key_pos <= last, part, MASKED)))
            if lo:
                scores.append((slot, 0, lo, score(q, x_ref[0, slot, 0:lo])))
        top = functools.reduce(
            jnp.maximum, [jnp.max(part, axis=1, keepdims=True) for _, _, _, part in scores]
        )
        total = jnp.zeros((tile, SLAB), jnp.float32)
        for slot, start, stop, part in scores:
            shift = top * scale - row_bias[slot_level(slot, tiers)]
            weight = jnp.exp2(part * scale - shift).astype(jnp.bfloat16)
            total = total + jnp.dot(
                weight, x_ref[0, slot, start:stop], preferred_element_type=jnp.float32
            )
        width = out_ref.shape[3]
        for slot in range(stride):
            rows = slice(slot * CHUNK, (slot + 1) * CHUNK)
            if slot < stride // 2:
                acc_ref[0, slot, lo:hi] = total[rows]
                peak_ref[0, slot, lo:hi] = jnp.broadcast_to(top[rows], (CHUNK, peak_ref.shape[3]))
            else:
                done = total[rows, :width] / total[rows, ONES_AT : ONES_AT + 1]
                out_ref[0, slot - stride // 2, lo:hi] = done.astype(jnp.bfloat16)


def earlier_kernel(tiers, group, info_ref, x_ref, acc_in, peak_in, *rest):
    extra_refs, (out_ref, acc, peak) = rest[:-3], rest[-3:]
    half, span = x_ref.shape[1:3]
    stride = 2 * half
    plane = info_ref[0] // group
    scale = HEAD_DIM ** (-0.5) * math.log2(math.e)
    depth = 2 * HEAD_DIM
    acc[...] = acc_in[0]
    peak[...] = peak_in[0]
    at = 0
    for tier in range(1, tiers):
        extras = extra_refs[at : at + 2 ** (tier - 1)]
        at += 2 ** (tier - 1)

        @pl.when(plane // 2 ** (tier - 1) % 2 == 1)
        def _():
            for q_slot in range(stride // 2**tier):
                q = query_part(x_ref[0, q_slot])[:, :depth]
                parts = [
                    (slot, ref, jnp.dot(q, ref[0, slot], preferred_element_type=jnp.float32))
                    for ref in extras
                    for slot in range(ref.shape[1])
                ]
                old = peak[q_slot][:, :1]
                top = functools.reduce(
                    jnp.maximum, [jnp.max(part, axis=1, keepdims=True) for _, _, part in parts], old
                )
                keep = jnp.exp2((old - top) * scale)
                numer = acc[q_slot, :, :128] * keep
                denom = acc[q_slot, :, ONES_AT : ONES_AT + 1] * keep
                for slot, ref, part in parts:
                    times = min(slot_level(q_slot, tiers), slot_level(slot, tiers)) - tier + 1
                    weight = jnp.exp2(part * scale - (top * scale - math.log2(times)))
                    denom = denom + jnp.sum(weight, axis=1, keepdims=True)
                    numer = (
                        numer
                        + lax.dot_general(
                            weight.astype(jnp.bfloat16),
                            ref[0, slot],
                            (((1,), (1,)), ((), ())),
                            preferred_element_type=jnp.float32,
                        )[:, :128]
                    )
                acc[q_slot, :, :128] = numer
                acc[q_slot, :, 128:] = jnp.broadcast_to(denom, (span, SLAB - 128))
                peak[q_slot] = jnp.broadcast_to(top, (span, peak.shape[2]))

    for slot in range(half):
        done = acc[slot, :, :128] / acc[slot, :, ONES_AT : ONES_AT + 1]
        out_ref[0, slot] = done.astype(jnp.bfloat16)


def attention(query_rows, key_rows, value_rows):
    rows, cols = query_rows.shape
    heads = cols // HEAD_DIM
    seq_count = lax.axis_size("seq")
    seq_pos = lax.axis_index("seq")
    total_rows = rows * seq_count
    tiers = 0
    while SEG0 * 2**tiers <= total_rows and total_rows % (SEG0 * 2**tiers) == 0:
        tiers += 1
    stride = 2 ** (tiers - 1)
    per = rows // stride
    group = SEG0 // rows
    heads_dev = heads // group
    span = SEG0 // stride

    packed = pl.pallas_call(
        functools.partial(pack_kernel, tiers),
        out_shape=jax.ShapeDtypeStruct((heads, stride, per, SLAB), jnp.bfloat16),
        in_specs=[pl.BlockSpec(memory_space=pltpu.VMEM)] * 3,
        out_specs=pl.BlockSpec(memory_space=pltpu.VMEM),
        compiler_params=pltpu.CompilerParams(vmem_limit_bytes=VMEM_BYTES),
        name="pack_heads",
    )(query_rows, key_rows, value_rows)

    groups = [[base + i for i in range(group)] for base in range(0, seq_count, group)]
    swapped = lax.all_to_all(
        packed.reshape(group, heads_dev, stride, per, SLAB), "seq", 0, 0, axis_index_groups=groups
    )
    local = swapped.transpose(1, 2, 0, 3, 4).reshape(heads_dev, stride, span, SLAB)

    half = stride // 2
    flat = local[:, :half, :, : 2 * HEAD_DIM].transpose(0, 1, 3, 2)
    extras = []
    for tier in range(1, tiers):
        bit = 2 ** (tier - 1)
        for twist in range(bit):
            pairs = [
                (i, ((i // group | bit) ^ twist) * group + i % group)
                for i in range(seq_count)
                if i // group & bit == 0
            ]
            extras.append(lax.ppermute(flat[:, : stride // 2**tier], "seq", pairs))

    info = seq_pos.reshape(1).astype(jnp.int32)
    smem = pl.BlockSpec(memory_space=pltpu.SMEM)

    def per_head(shape):
        return pl.BlockSpec((1,) + tuple(shape[1:]), lambda h: (h,) + (0,) * (len(shape) - 1))

    upper_shape = (heads_dev, stride - half, span, 128)
    acc_shape = (heads_dev, half, span, SLAB)
    peak_shape = (heads_dev, half, span, 128)
    upper, acc, peak = pl.pallas_call(
        functools.partial(segment_kernel, tiers, heads_dev, group),
        grid=(heads_dev,),
        out_shape=(
            jax.ShapeDtypeStruct(upper_shape, jnp.bfloat16),
            jax.ShapeDtypeStruct(acc_shape, jnp.float32),
            jax.ShapeDtypeStruct(peak_shape, jnp.float32),
        ),
        in_specs=[smem, per_head(local.shape)],
        out_specs=(per_head(upper_shape), per_head(acc_shape), per_head(peak_shape)),
        compiler_params=pltpu.CompilerParams(vmem_limit_bytes=VMEM_BYTES),
        cost_estimate=pl.CostEstimate(
            flops=heads_dev * SEG0 * SEG0 * 4 * SLAB,
            bytes_accessed=heads_dev * SEG0 * SLAB * 6,
            transcendentals=heads_dev * SEG0 * SEG0,
        ),
        name="segment_attend",
    )(info, local)

    groups = [[base + i for i in range(group)] for base in range(0, seq_count, group)]

    def send_home(part):
        part = part[..., :HEAD_DIM].reshape(heads_dev, -1, group, per, HEAD_DIM)
        part = part.transpose(2, 0, 1, 4, 3)
        part = lax.all_to_all(part, "seq", 0, 0, axis_index_groups=groups)
        return part.reshape(heads, -1, HEAD_DIM, per)

    upper_home = send_home(upper)
    lower = pl.pallas_call(
        functools.partial(earlier_kernel, tiers, group),
        grid=(heads_dev,),
        out_shape=jax.ShapeDtypeStruct(peak_shape, jnp.bfloat16),
        in_specs=[smem, pl.BlockSpec((1, half, span, SLAB), lambda h: (h, 0, 0, 0))]
        + [per_head(acc_shape), per_head(peak_shape)]
        + [per_head(extra.shape) for extra in extras],
        out_specs=per_head(peak_shape),
        scratch_shapes=[
            pltpu.VMEM((half, span, SLAB), jnp.float32),
            pltpu.VMEM((half, span, 128), jnp.float32),
        ],
        compiler_params=pltpu.CompilerParams(vmem_limit_bytes=VMEM_BYTES),
        name="earlier_segments",
    )(info, local, acc, peak, *extras)
    home = jnp.concatenate([send_home(lower), upper_home], axis=1)
    ordered = []
    for head in range(heads):
        order = [reversed_bits(res ^ head % stride, tiers - 1) for res in range(stride)]
        ordered.append(jnp.stack([home[head, slot] for slot in order]))
    whole = jnp.stack(ordered)
    return whole.transpose(3, 1, 0, 2).reshape(rows, cols)


def lift_kernel(att_ref, states_ref, proj_ref, gain_ref, up_ref, resid_ref, hidden_ref, normed):
    @pl.when(pl.program_id(0) == 0)
    def _():
        projected = jnp.dot(att_ref[...], proj_ref[...], preferred_element_type=jnp.float32)
        resid = (states_ref[...].astype(jnp.float32) + projected).astype(jnp.bfloat16)
        resid_ref[...] = resid
        wide = resid.astype(jnp.float32)
        centered = wide - jnp.mean(wide, axis=1, keepdims=True)
        var = jnp.mean(centered * centered, axis=1, keepdims=True)
        normed[...] = (centered * lax.rsqrt(var + 1e-05) * gain_ref[...]).astype(jnp.bfloat16)

    raw = jnp.dot(normed[...], up_ref[...], preferred_element_type=jnp.float32)
    hidden_ref[...] = (0.5 * raw * (1.0 + lax.erf(raw * math.sqrt(0.5)))).astype(jnp.bfloat16)


def lower_kernel(info_ref, hidden_ref, mine_ref, other_ref, resid_ref, out_ref):
    hidden = hidden_ref[...]

    def product(ref):
        count, cols, depth = ref.shape
        return lax.dot_general(
            hidden,
            ref[...].reshape(count * cols, depth),
            (((1,), (1,)), ((), ())),
            preferred_element_type=jnp.float32,
        )

    mine, other = product(mine_ref), product(other_ref)
    is_first = info_ref[0] % 2 == 0
    pair = (jnp.where(is_first, mine, other), jnp.where(is_first, other, mine))
    cols = mine_ref.shape[1]
    mixed = jnp.concatenate(
        [part[:, i * cols : (i + 1) * cols] for i in range(mine_ref.shape[0]) for part in pair], axis=1
    )
    out_ref[...] = (resid_ref[...].astype(jnp.float32) + mixed).astype(jnp.bfloat16)


def feed_forward(attended, states, out_proj, norm_gain, up_proj, down_mine):
    rows, width = states.shape
    units = up_proj.shape[1]
    step = math.gcd(units, 512)
    whole = lambda i: (0, 0)
    seq_count = lax.axis_size("seq")
    attended, down_mine = lax.optimization_barrier((attended, down_mine))
    down_other = lax.ppermute(down_mine, "seq", [(i, i ^ 1) for i in range(seq_count)])
    resid, hidden = pl.pallas_call(
        lift_kernel,
        grid=(units // step,),
        out_shape=(
            jax.ShapeDtypeStruct((rows, width), jnp.bfloat16),
            jax.ShapeDtypeStruct((rows, units), jnp.bfloat16),
        ),
        in_specs=[
            pl.BlockSpec(attended.shape, whole),
            pl.BlockSpec((rows, width), whole),
            pl.BlockSpec(out_proj.shape, whole),
            pl.BlockSpec((1, width), whole),
            pl.BlockSpec((width, step), lambda i: (0, i)),
        ],
        out_specs=(
            pl.BlockSpec((rows, width), whole),
            pl.BlockSpec((rows, step), lambda i: (0, i)),
        ),
        scratch_shapes=[pltpu.VMEM((rows, width), jnp.bfloat16)],
        compiler_params=pltpu.CompilerParams(vmem_limit_bytes=VMEM_BYTES),
        cost_estimate=pl.CostEstimate(
            flops=2 * rows * width * (units + attended.shape[1]),
            bytes_accessed=2 * width * (units + attended.shape[1]),
            transcendentals=rows * units,
        ),
        name="project_and_lift",
    )(attended, states, out_proj, norm_gain.reshape(1, width), up_proj)
    pairs = seq_count // 2
    cols = width // seq_count
    take = next(n for n in range(1, pairs + 1) if pairs % n == 0 and 2 * n * cols % 128 == 0)
    weights = pl.BlockSpec((take, cols, units), lambda i: (i, 0, 0))
    part = pl.BlockSpec((rows, 2 * take * cols), lambda i: (0, i))
    return pl.pallas_call(
        lower_kernel,
        grid=(pairs // take,),
        out_shape=jax.ShapeDtypeStruct((rows, width), jnp.bfloat16),
        in_specs=[
            pl.BlockSpec(memory_space=pltpu.SMEM),
            pl.BlockSpec((rows, units), whole),
            weights,
            weights,
            part,
        ],
        out_specs=part,
        compiler_params=pltpu.CompilerParams(vmem_limit_bytes=VMEM_BYTES),
        name="lower",
    )(lax.axis_index("seq").reshape(1).astype(jnp.int32), hidden, down_mine, down_other, resid)


def per_device(states, query_rows, key_rows, value_rows, out_proj, norm_gain, up_proj, down_proj):
    model_width = states.shape[1]
    mp_pos = lax.axis_index("mp")
    if lax.axis_size("mp") == 1:
        same_core = [list(range(core, lax.axis_size("seq"), 2)) for core in range(2)]
        down_mine = lax.all_gather(down_proj.T, "seq", axis=0, axis_index_groups=same_core)
        attended = attention(query_rows, key_rows, value_rows)
        return feed_forward(attended, states, out_proj, norm_gain, up_proj, down_mine)
    down_rows = lax.all_gather(down_proj.T, "seq", axis=0, tiled=True)
    attended = attention(query_rows, key_rows, value_rows)
    projected = jnp.dot(attended, out_proj, preferred_element_type=jnp.float32)
    share = lax.psum_scatter(projected, "mp", scatter_dimension=1, tiled=True)
    half_width = share.shape[1]
    states_share = lax.dynamic_slice_in_dim(states, mp_pos * half_width, half_width, 1)
    resid_share = (states_share.astype(jnp.float32) + share).astype(jnp.bfloat16)
    share_wide = resid_share.astype(jnp.float32)
    part_sum, part_squares = lax.psum(
        (
            jnp.sum(share_wide, axis=1, keepdims=True),
            jnp.sum(share_wide * share_wide, axis=1, keepdims=True),
        ),
        "mp",
    )
    row_mean = part_sum / model_width
    row_var = part_squares / model_width - row_mean * row_mean
    gain_share = lax.dynamic_slice_in_dim(norm_gain, mp_pos * half_width, half_width, 0)
    normed_share = (
        (share_wide - row_mean) * lax.rsqrt(row_var + 1e-05) * gain_share[None, :]
    ).astype(jnp.bfloat16)
    normed = lax.all_gather(normed_share, "mp", axis=1, tiled=True)
    hidden = jax.nn.gelu(
        jnp.dot(normed, up_proj, preferred_element_type=jnp.float32), approximate=False
    ).astype(jnp.bfloat16)
    terms = lax.dot_general(
        hidden, down_rows, (((1,), (1,)), ((), ())), preferred_element_type=jnp.float32
    )
    ffn_part = lax.psum_scatter(
        terms.astype(jnp.bfloat16), "mp", scatter_dimension=1, tiled=True
    ).astype(jnp.float32)
    return (resid_share.astype(jnp.float32) + ffn_part).astype(jnp.bfloat16)


def solution(mesh):
    in_specs = (
        P("seq", None),
        P("seq", "mp"),
        P("seq", "mp"),
        P("seq", "mp"),
        P("mp", None),
        P(),
        P(None, "mp"),
        P("mp", "seq"),
    )
    out_specs = P("seq", "mp")
    return jax.shard_map(
        per_device, mesh=mesh, in_specs=in_specs, out_specs=out_specs, check_vma=False
    )
```

```python
import functools
import math

import jax
import jax.numpy as jnp
from jax import lax
from jax.experimental import pallas as pl
from jax.experimental.pallas import tpu as pltpu
from jax.sharding import PartitionSpec as P

HEAD_DIM = 80
SEG0 = 2048
SLAB = 256
ONES_AT = 3 * HEAD_DIM
CHUNK = 128
MASKED = -1e30
VMEM_BYTES = 30 * 1024 * 1024
PARTS = 2


def reversed_bits(value, bits):
    return sum((value >> b & 1) << (bits - 1 - b) for b in range(bits))


def slot_level(slot, tiers):
    return tiers - 1 - slot.bit_length()


def pack_kernel(tiers, q_ref, k_ref, v_ref, out_ref):
    stride = 2 ** (tiers - 1)
    rows = q_ref.shape[0]
    per = rows // stride
    place = lax.broadcasted_iota(jnp.int32, (rows, rows), 0)
    source = lax.broadcasted_iota(jnp.int32, (rows, rows), 1)
    wanted = (place & (per - 1)) * stride + (place >> (per.bit_length() - 1))
    perm = (wanted == source).astype(jnp.bfloat16)
    sorted_rows = [
        jnp.dot(perm, ref[...], preferred_element_type=jnp.float32) for ref in (v_ref, k_ref, q_ref)
    ]
    ones = jnp.ones((rows, SLAB - ONES_AT), jnp.float32)
    for head in range(out_ref.shape[0]):
        cols = slice(head * HEAD_DIM, (head + 1) * HEAD_DIM)
        slab = jnp.concatenate([part[:, cols] for part in sorted_rows] + [ones], axis=1).astype(
            jnp.bfloat16
        )
        for slot in range(stride):
            res = reversed_bits(slot, tiers - 1) ^ head % stride
            out_ref[head, slot] = slab[res * per : (res + 1) * per]


def query_part(rows):
    sel_row = lax.broadcasted_iota(jnp.int32, (SLAB, SLAB), 0)
    sel_col = lax.broadcasted_iota(jnp.int32, (SLAB, SLAB), 1)
    to_keys = ((sel_row == sel_col + HEAD_DIM) & (sel_row >= 2 * HEAD_DIM) & (sel_row < ONES_AT)).astype(
        jnp.bfloat16
    )
    return jnp.dot(rows, to_keys, preferred_element_type=jnp.float32).astype(jnp.bfloat16)


def segment_kernel(tiers, heads_dev, group, info_ref, x_ref, out_ref, acc_ref, peak_ref):
    stride = 2 ** (tiers - 1)
    span = x_ref.shape[2]
    seq_pos = info_ref[0]
    head_class = (seq_pos % group * heads_dev + pl.program_id(0)) % stride
    scale = HEAD_DIM ** (-0.5) * math.log2(math.e)

    def score(q, keys):
        return lax.dot_general(q, keys, (((1,), (1,)), ((), ())), preferred_element_type=jnp.float32)

    tile = stride * CHUNK
    row_ids = lax.broadcasted_iota(jnp.int32, (tile, 1), 0)
    row_slot = row_ids // CHUNK
    row_pos = row_ids % CHUNK
    row_res = jnp.zeros_like(row_ids)
    row_level = jnp.zeros_like(row_ids)
    for slot in range(stride):
        row_res = jnp.where(row_slot == slot, reversed_bits(slot, tiers - 1) ^ head_class, row_res)
        row_level = jnp.where(row_slot == slot, slot_level(slot, tiers), row_level)
    row_bias = []
    for level in range(tiers):
        count = jnp.minimum(row_level, level) + 1
        bias = jnp.zeros((tile, 1), jnp.float32)
        for times in range(2, tiers + 1):
            bias = jnp.where(count == times, math.log2(times), bias)
        row_bias.append(bias)
    key_pos = lax.broadcasted_iota(jnp.int32, (tile, CHUNK), 1)

    for chunk in range(span // CHUNK):
        lo, hi = chunk * CHUNK, (chunk + 1) * CHUNK
        q = query_part(jnp.concatenate([x_ref[0, slot, lo:hi] for slot in range(stride)], axis=0))
        scores = []
        for slot in range(stride):
            key_res = reversed_bits(slot, tiers - 1) ^ head_class
            last = row_pos - (key_res > row_res).astype(jnp.int32)
            part = score(q, x_ref[0, slot, lo:hi])
            scores.append((slot, lo, hi, jnp.where(key_pos <= last, part, MASKED)))
            if lo:
                scores.append((slot, 0, lo, score(q, x_ref[0, slot, 0:lo])))
        top = functools.reduce(
            jnp.maximum, [jnp.max(part, axis=1, keepdims=True) for _, _, _, part in scores]
        )
        total = jnp.zeros((tile, SLAB), jnp.float32)
        for slot, start, stop, part in scores:
            shift = top * scale - row_bias[slot_level(slot, tiers)]
            weight = jnp.exp2(part * scale - shift).astype(jnp.bfloat16)
            total = total + jnp.dot(
                weight, x_ref[0, slot, start:stop], preferred_element_type=jnp.float32
            )
        width = out_ref.shape[3]
        for slot in range(stride):
            rows = slice(slot * CHUNK, (slot + 1) * CHUNK)
            if slot < stride // 2:
                acc_ref[0, slot, lo:hi] = total[rows]
                peak_ref[0, slot, lo:hi] = jnp.broadcast_to(top[rows], (CHUNK, peak_ref.shape[3]))
            else:
                done = total[rows, :width] / total[rows, ONES_AT : ONES_AT + 1]
                out_ref[0, slot - stride // 2, lo:hi] = done.astype(jnp.bfloat16)


def earlier_kernel(tiers, group, info_ref, x_ref, acc_in, peak_in, *rest):
    extra_refs, (out_ref, acc, peak) = rest[:-3], rest[-3:]
    half, span = x_ref.shape[1:3]
    stride = 2 * half
    plane = info_ref[0] // group
    scale = HEAD_DIM ** (-0.5) * math.log2(math.e)
    depth = 2 * HEAD_DIM
    acc[...] = acc_in[0]
    peak[...] = peak_in[0]
    at = 0
    for tier in range(1, tiers):
        extras = extra_refs[at : at + 2 ** (tier - 1)]
        at += 2 ** (tier - 1)

        @pl.when(plane // 2 ** (tier - 1) % 2 == 1)
        def _():
            for q_slot in range(stride // 2**tier):
                q = query_part(x_ref[0, q_slot])[:, :depth]
                parts = [
                    (slot, ref, jnp.dot(q, ref[0, slot], preferred_element_type=jnp.float32))
                    for ref in extras
                    for slot in range(ref.shape[1])
                ]
                old = peak[q_slot][:, :1]
                top = functools.reduce(
                    jnp.maximum, [jnp.max(part, axis=1, keepdims=True) for _, _, part in parts], old
                )
                keep = jnp.exp2((old - top) * scale)
                numer = acc[q_slot, :, :128] * keep
                denom = acc[q_slot, :, ONES_AT : ONES_AT + 1] * keep
                for slot, ref, part in parts:
                    times = min(slot_level(q_slot, tiers), slot_level(slot, tiers)) - tier + 1
                    weight = jnp.exp2(part * scale - (top * scale - math.log2(times)))
                    denom = denom + jnp.sum(weight, axis=1, keepdims=True)
                    numer = (
                        numer
                        + lax.dot_general(
                            weight.astype(jnp.bfloat16),
                            ref[0, slot],
                            (((1,), (1,)), ((), ())),
                            preferred_element_type=jnp.float32,
                        )[:, :128]
                    )
                acc[q_slot, :, :128] = numer
                acc[q_slot, :, 128:] = jnp.broadcast_to(denom, (span, SLAB - 128))
                peak[q_slot] = jnp.broadcast_to(top, (span, peak.shape[2]))

    for slot in range(half):
        done = acc[slot, :, :128] / acc[slot, :, ONES_AT : ONES_AT + 1]
        out_ref[0, slot] = done.astype(jnp.bfloat16)


def attention(query_rows, key_rows, value_rows):
    rows, cols = query_rows.shape
    heads = cols // HEAD_DIM
    seq_count = lax.axis_size("seq")
    seq_pos = lax.axis_index("seq")
    total_rows = rows * seq_count
    tiers = 0
    while SEG0 * 2**tiers <= total_rows and total_rows % (SEG0 * 2**tiers) == 0:
        tiers += 1
    stride = 2 ** (tiers - 1)
    per = rows // stride
    group = SEG0 // rows
    heads_dev = heads // group
    span = SEG0 // stride

    packed = pl.pallas_call(
        functools.partial(pack_kernel, tiers),
        out_shape=jax.ShapeDtypeStruct((heads, stride, per, SLAB), jnp.bfloat16),
        in_specs=[pl.BlockSpec(memory_space=pltpu.VMEM)] * 3,
        out_specs=pl.BlockSpec(memory_space=pltpu.VMEM),
        compiler_params=pltpu.CompilerParams(vmem_limit_bytes=VMEM_BYTES),
        name="pack_heads",
    )(query_rows, key_rows, value_rows)

    groups = [[base + i for i in range(group)] for base in range(0, seq_count, group)]
    swapped = lax.all_to_all(
        packed.reshape(group, heads_dev, stride, per, SLAB), "seq", 0, 0, axis_index_groups=groups
    )
    local = swapped.transpose(1, 2, 0, 3, 4).reshape(heads_dev, stride, span, SLAB)

    half = stride // 2
    flat = local[:, :half, :, : 2 * HEAD_DIM].transpose(0, 1, 3, 2)
    extras = []
    for tier in range(1, tiers):
        bit = 2 ** (tier - 1)
        for twist in range(bit):
            pairs = [
                (i, ((i // group | bit) ^ twist) * group + i % group)
                for i in range(seq_count)
                if i // group & bit == 0
            ]
            extras.append(lax.ppermute(flat[:, : stride // 2**tier], "seq", pairs))

    info = seq_pos.reshape(1).astype(jnp.int32)
    smem = pl.BlockSpec(memory_space=pltpu.SMEM)

    def per_head(shape):
        return pl.BlockSpec((1,) + tuple(shape[1:]), lambda h: (h,) + (0,) * (len(shape) - 1))

    upper_shape = (heads_dev, stride - half, span, 128)
    acc_shape = (heads_dev, half, span, SLAB)
    peak_shape = (heads_dev, half, span, 128)
    upper, acc, peak = pl.pallas_call(
        functools.partial(segment_kernel, tiers, heads_dev, group),
        grid=(heads_dev,),
        out_shape=(
            jax.ShapeDtypeStruct(upper_shape, jnp.bfloat16),
            jax.ShapeDtypeStruct(acc_shape, jnp.float32),
            jax.ShapeDtypeStruct(peak_shape, jnp.float32),
        ),
        in_specs=[smem, per_head(local.shape)],
        out_specs=(per_head(upper_shape), per_head(acc_shape), per_head(peak_shape)),
        compiler_params=pltpu.CompilerParams(vmem_limit_bytes=VMEM_BYTES),
        cost_estimate=pl.CostEstimate(
            flops=heads_dev * SEG0 * SEG0 * 4 * SLAB,
            bytes_accessed=heads_dev * SEG0 * SLAB * 6,
            transcendentals=heads_dev * SEG0 * SEG0,
        ),
        name="segment_attend",
    )(info, local)

    groups = [[base + i for i in range(group)] for base in range(0, seq_count, group)]

    def send_home(part):
        part = part[..., :HEAD_DIM].reshape(heads_dev, -1, group, per, HEAD_DIM)
        part = part.transpose(2, 0, 1, 4, 3)
        part = lax.all_to_all(part, "seq", 0, 0, axis_index_groups=groups)
        return part.reshape(heads, -1, HEAD_DIM, per)

    upper_home = send_home(upper)
    lower = pl.pallas_call(
        functools.partial(earlier_kernel, tiers, group),
        grid=(heads_dev,),
        out_shape=jax.ShapeDtypeStruct(peak_shape, jnp.bfloat16),
        in_specs=[smem, pl.BlockSpec((1, half, span, SLAB), lambda h: (h, 0, 0, 0))]
        + [per_head(acc_shape), per_head(peak_shape)]
        + [per_head(extra.shape) for extra in extras],
        out_specs=per_head(peak_shape),
        scratch_shapes=[
            pltpu.VMEM((half, span, SLAB), jnp.float32),
            pltpu.VMEM((half, span, 128), jnp.float32),
        ],
        compiler_params=pltpu.CompilerParams(vmem_limit_bytes=VMEM_BYTES),
        name="earlier_segments",
    )(info, local, acc, peak, *extras)
    home = jnp.concatenate([send_home(lower), upper_home], axis=1)
    ordered = []
    for head in range(heads):
        order = [reversed_bits(res ^ head % stride, tiers - 1) for res in range(stride)]
        ordered.append(jnp.stack([home[head, slot] for slot in order]))
    whole = jnp.stack(ordered)
    return whole.transpose(3, 1, 0, 2).reshape(rows, cols)


def lift_kernel(att_ref, states_ref, proj_ref, gain_ref, up_ref, resid_ref, hidden_ref, normed):
    @pl.when(pl.program_id(0) == 0)
    def _():
        projected = jnp.dot(att_ref[...], proj_ref[...], preferred_element_type=jnp.float32)
        resid = (states_ref[...].astype(jnp.float32) + projected).astype(jnp.bfloat16)
        resid_ref[...] = resid
        wide = resid.astype(jnp.float32)
        centered = wide - jnp.mean(wide, axis=1, keepdims=True)
        var = jnp.mean(centered * centered, axis=1, keepdims=True)
        normed[...] = (centered * lax.rsqrt(var + 1e-05) * gain_ref[...]).astype(jnp.bfloat16)

    raw = jnp.dot(normed[...], up_ref[...], preferred_element_type=jnp.float32)
    hidden_ref[...] = (0.5 * raw * (1.0 + lax.erf(raw * math.sqrt(0.5)))).astype(jnp.bfloat16)


def lower_kernel(hidden_ref, down_ref, before_ref, out_ref):
    mixed = lax.dot_general(
        hidden_ref[...],
        down_ref[...],
        (((1,), (1,)), ((), ())),
        preferred_element_type=jnp.float32,
    )
    out_ref[...] = (before_ref[...].astype(jnp.float32) + mixed).astype(out_ref.dtype)


def feed_forward(attended, states, out_proj, norm_gain, up_proj, down_parts):
    rows, width = states.shape
    units = up_proj.shape[1]
    step = math.gcd(units, 512)
    whole = lambda i: (0, 0)
    resid, hidden = pl.pallas_call(
        lift_kernel,
        grid=(units // step,),
        out_shape=(
            jax.ShapeDtypeStruct((rows, width), jnp.bfloat16),
            jax.ShapeDtypeStruct((rows, units), jnp.bfloat16),
        ),
        in_specs=[
            pl.BlockSpec(attended.shape, whole),
            pl.BlockSpec((rows, width), whole),
            pl.BlockSpec(out_proj.shape, whole),
            pl.BlockSpec((1, width), whole),
            pl.BlockSpec((width, step), lambda i: (0, i)),
        ],
        out_specs=(
            pl.BlockSpec((rows, width), whole),
            pl.BlockSpec((rows, step), lambda i: (0, i)),
        ),
        scratch_shapes=[pltpu.VMEM((rows, width), jnp.bfloat16)],
        compiler_params=pltpu.CompilerParams(vmem_limit_bytes=VMEM_BYTES),
        cost_estimate=pl.CostEstimate(
            flops=2 * rows * width * (units + attended.shape[1]),
            bytes_accessed=2 * width * (units + attended.shape[1]),
            transcendentals=rows * units,
        ),
        name="project_and_lift",
    )(attended, states, out_proj, norm_gain.reshape(1, width), up_proj)
    part = math.gcd(width, 256)
    total, start = resid, 0
    for down_part in down_parts:
        depth = down_part.shape[1]
        last = start + depth == units
        block, kept = start // depth, jnp.bfloat16 if last else jnp.float32
        total = pl.pallas_call(
            lower_kernel,
            grid=(width // part,),
            out_shape=jax.ShapeDtypeStruct((rows, width), kept),
            in_specs=[
                pl.BlockSpec((rows, depth), lambda i, block=block: (0, block)),
                pl.BlockSpec((part, depth), lambda i: (i, 0)),
                pl.BlockSpec((rows, part), lambda i: (0, i)),
            ],
            out_specs=pl.BlockSpec((rows, part), lambda i: (0, i)),
            compiler_params=pltpu.CompilerParams(vmem_limit_bytes=VMEM_BYTES),
            cost_estimate=pl.CostEstimate(
                flops=2 * rows * width * depth, bytes_accessed=2 * width * depth, transcendentals=0
            ),
            name="lower",
        )(hidden, down_part, total)
        start += depth
    return total


def per_device(states, query_rows, key_rows, value_rows, out_proj, norm_gain, up_proj, down_proj):
    model_width = states.shape[1]
    mp_pos = lax.axis_index("mp")
    if lax.axis_size("mp") == 1:
        depth = down_proj.shape[0]
        parts = PARTS if depth % (PARTS * 128) == 0 else 1
        down_parts = [
            lax.all_gather(rows, "seq", axis=0, tiled=True)
            for rows in jnp.split(down_proj.T, parts, axis=1)
        ]
        attended = attention(query_rows, key_rows, value_rows)
        return feed_forward(attended, states, out_proj, norm_gain, up_proj, down_parts)
    down_rows = lax.all_gather(down_proj.T, "seq", axis=0, tiled=True)
    attended = attention(query_rows, key_rows, value_rows)
    projected = jnp.dot(attended, out_proj, preferred_element_type=jnp.float32)
    share = lax.psum_scatter(projected, "mp", scatter_dimension=1, tiled=True)
    half_width = share.shape[1]
    states_share = lax.dynamic_slice_in_dim(states, mp_pos * half_width, half_width, 1)
    resid_share = (states_share.astype(jnp.float32) + share).astype(jnp.bfloat16)
    share_wide = resid_share.astype(jnp.float32)
    part_sum, part_squares = lax.psum(
        (
            jnp.sum(share_wide, axis=1, keepdims=True),
            jnp.sum(share_wide * share_wide, axis=1, keepdims=True),
        ),
        "mp",
    )
    row_mean = part_sum / model_width
    row_var = part_squares / model_width - row_mean * row_mean
    gain_share = lax.dynamic_slice_in_dim(norm_gain, mp_pos * half_width, half_width, 0)
    normed_share = (
        (share_wide - row_mean) * lax.rsqrt(row_var + 1e-05) * gain_share[None, :]
    ).astype(jnp.bfloat16)
    normed = lax.all_gather(normed_share, "mp", axis=1, tiled=True)
    hidden = jax.nn.gelu(
        jnp.dot(normed, up_proj, preferred_element_type=jnp.float32), approximate=False
    ).astype(jnp.bfloat16)
    terms = lax.dot_general(
        hidden, down_rows, (((1,), (1,)), ((), ())), preferred_element_type=jnp.float32
    )
    ffn_part = lax.psum_scatter(
        terms.astype(jnp.bfloat16), "mp", scatter_dimension=1, tiled=True
    ).astype(jnp.float32)
    return (resid_share.astype(jnp.float32) + ffn_part).astype(jnp.bfloat16)


def solution(mesh):
    in_specs = (
        P("seq", None),
        P("seq", "mp"),
        P("seq", "mp"),
        P("seq", "mp"),
        P("mp", None),
        P(),
        P(None, "mp"),
        P("mp", "seq"),
    )
    out_specs = P("seq", "mp")
    return jax.shard_map(
        per_device, mesh=mesh, in_specs=in_specs, out_specs=out_specs, check_vma=False
    )
```
